512 devices in a mesh: section: 16 (over y, core), dp: 32 (over x, z).
Axes of the slice: x: 4, y: 8, z: 8, core: 2. Of those that a mesh axis runs over, the one named last changes fastest.
Arguments:
- hidden_in: bfloat16 [16, 4096, 8192], P('section', 'dp'), may hold values from -50 to 50
- key_grad: bfloat16 [16, 4096, 1024], P('section', 'dp'), may hold values from -6 to 6
- key_weight: bfloat16 [16, 8192, 1024], P('section', 'dp'), may hold values from -0.1875 to 0.1875
- adapter_a: bfloat16 [16, 64, 8192], P('section', None, 'dp'), may hold values from -0.75 to 0.75
- adapter_b: bfloat16 [16, 64, 1024], P('section'), may hold values from -0.1875 to 0.1875
- norm_gain: float32 [16, 8192], P('section'), may hold values from 0.1 to 1.9
- keep_flags: int32 [16], P('section'), may hold values from 0 to 1, as said below
- valid_counts: int32 [32], P('dp'), may hold values from 32 to 128, as said below
Outputs:
- grad_stream: bfloat16 [16, 4096, 8192], P('section', 'dp')
- grad_adapter_a: float32 [16, 64, 8192], P('section', None, 'dp')
- grad_adapter_b: float32 [16, 64, 1024], P('section', None, 'dp')
The draws below stay inside these ranges and needn't reach their ends.
Inputs may be any that keep to these rules, and one draw needn't show every extreme that they name: `keep_flags`: some kept layer has the layer 8 positions away (cyclically) dropped. `valid_counts`: the first that many rows of a replica are live; at least one replica has all 128 live.
All inputs are finite; a program needn't handle non-finite values.
Results may differ from the reference program's by a relative error of at most 0.02.
Values may be sent and summed in bfloat16 or wider, within the bound.
No kernel may reach another device: no remote copies, remote signals or barrier semaphores. Data moves between devices by JAX's collectives and lax.ppermute only.
A program may use at most 128 MiB of HBM per device.

```python
import math
import jax
import jax.numpy as jnp
from jax import lax

D = 8192
KV = 1024
RANK = 64
TOK_DEV = 128
TOKEN_SLOTS = 4096
LAYERS = 16
REPLICAS = 32


def draw_hidden_in(key, part):
    key = jax.random.fold_in(key, 11)
    first_key, second_key = jax.random.split(key)
    shape = (LAYERS, TOKEN_SLOTS, D)
    base = jnp.clip(jax.random.normal(first_key, shape, jnp.float32), -5.0, 5.0)
    scales = jnp.exp(jax.random.uniform(second_key, (LAYERS, TOKEN_SLOTS, 1), jnp.float32, 0.0, math.log(10.0)))
    return (base * scales).astype(jnp.bfloat16)


def draw_keep_flags(key, part):
    key = jax.random.fold_in(key, 12)
    first_key, second_key = jax.random.split(key)
    flags = jax.random.randint(first_key, (LAYERS,), 0, 2)
    chosen = jax.random.randint(second_key, (), 0, LAYERS)
    slots = jnp.arange(LAYERS, dtype=jnp.int32)
    flags = jnp.where(slots == chosen, 1, flags)
    flags = jnp.where(slots == (chosen + LAYERS // 2) % LAYERS, 0, flags)
    return flags.astype(jnp.int32)


def draw_valid_counts(key, part):
    key = jax.random.fold_in(key, 13)
    first_key, second_key = jax.random.split(key)
    counts = jax.random.randint(first_key, (REPLICAS,), TOK_DEV // 4, TOK_DEV + 1)
    chosen = jax.random.randint(second_key, (), 0, REPLICAS)
    slots = jnp.arange(REPLICAS, dtype=jnp.int32)
    return jnp.where(slots == chosen, TOK_DEV, counts).astype(jnp.int32)


def level_of(stream_key, dims, cuts, low, high):
    loudness = 1.0
    for axis_at, parts in cuts:
        heights = jax.random.uniform(jax.random.fold_in(jax.random.fold_in(stream_key, 6), axis_at), (parts,), jnp.float32, low / len(cuts), high / len(cuts))
        loudness = loudness * jnp.repeat(jnp.exp(heights), dims[axis_at] // parts).reshape((-1,) + (1,) * (len(dims) - 1 - axis_at))
    return loudness


def bell_draw(key, shape, spread, limit, cuts=(), kind=jnp.bfloat16):
    drawn = jax.random.normal(key, shape, jnp.float32) * spread
    if len(cuts) > 0:
        drawn = level_of(key, shape, cuts, -0.22, 0.18) * drawn
    return jnp.clip(drawn, min=-limit, max=limit).astype(kind)


def setup_inputs(seed: int = 0) -> dict:
    keys = jax.random.split(jax.random.key(seed), 9)
    return {
        "hidden_in": draw_hidden_in(jax.random.fold_in(keys[8], 71), 0),
        "key_grad": bell_draw(keys[1], (LAYERS, TOKEN_SLOTS, KV), 1.0, 6.0, ((0, 16), (1, 32))),
        "key_weight": bell_draw(keys[2], (LAYERS, D, KV), KV ** -0.5, 0.1875, ((0, 16), (1, 32))),
        "adapter_a": bell_draw(keys[3], (LAYERS, RANK, D), RANK ** -0.5, 0.75, ((0, 16), (2, 32))),
        "adapter_b": bell_draw(keys[4], (LAYERS, RANK, KV), KV ** -0.5, 0.1875, ((0, 16),)),
        "norm_gain": jnp.clip(1.0 + 0.18 * jax.random.normal(keys[5], (LAYERS, D), jnp.float32), 0.1, 1.9),
        "keep_flags": draw_keep_flags(jax.random.fold_in(keys[8], 71), 0),
        "valid_counts": draw_valid_counts(jax.random.fold_in(keys[8], 71), 0),
    }


ADAPTER_SCALING = 0.5
EPS = 1e-06

def contract_final_axis(left, right):
    return lax.dot_general(left, right, (((1,), (1,)), ((), ())), preferred_element_type=jnp.float32)

def contract_first(left, right):
    return lax.dot_general(left, right, (((0,), (0,)), ((), ())), preferred_element_type=jnp.float32)

def reference(hidden_in, key_grad, key_weight, adapter_a, adapter_b, norm_gain, keep_flags, valid_counts):
    token_ids = jnp.arange(TOKEN_SLOTS, dtype=jnp.int32)
    replica_of = (token_ids // TOK_DEV).astype(jnp.int32)
    live_tok = token_ids % TOK_DEV < valid_counts[replica_of]
    scale_factor = ADAPTER_SCALING / math.sqrt(TOKEN_SLOTS)

    def layer_step(carry, layer):
        stream_in, key_raw, frozen_weight, a_mat, b_mat, gain_row, keep = layer
        live_rows = (live_tok & (keep > 0))[:, None]
        masked_gradient = jnp.where(live_rows, key_raw, jnp.zeros_like(key_raw))
        lowrank_projection = contract_final_axis(masked_gradient, b_mat).astype(jnp.bfloat16)
        normed_gradient = (contract_final_axis(masked_gradient, frozen_weight) + ADAPTER_SCALING * jnp.dot(lowrank_projection, a_mat, preferred_element_type=jnp.float32)).astype(jnp.bfloat16)
        resid = stream_in.astype(jnp.float32)
        inv_rms = lax.rsqrt(lax.optimization_barrier(jnp.mean(resid * resid, axis=1, keepdims=True)) + EPS)
        normed = (resid * inv_rms * gain_row).astype(jnp.bfloat16)
        slope_rows = gain_row * normed_gradient.astype(jnp.float32)
        inner_mean = lax.optimization_barrier(jnp.mean(resid * slope_rows, axis=1, keepdims=True))
        grad_term = (inv_rms * (slope_rows - resid * inv_rms * inv_rms * inner_mean)).astype(jnp.bfloat16)
        projected = contract_final_axis(normed, a_mat).astype(jnp.bfloat16)
        grad_a = scale_factor * contract_first(lowrank_projection, normed)
        grad_b = scale_factor * contract_first(projected, masked_gradient)
        stream = (carry.astype(jnp.float32) + grad_term.astype(jnp.float32)).astype(jnp.bfloat16)
        return (stream, (stream, grad_a, grad_b))
    start = jnp.zeros((TOKEN_SLOTS, D), jnp.bfloat16)
    layers = (hidden_in, key_grad, key_weight, adapter_a, adapter_b, norm_gain, keep_flags)
    last_carry, outputs = lax.scan(layer_step, start, layers, reverse=True)
    return (outputs[0], outputs[1], outputs[2])
```

```python
import math

import jax
import jax.numpy as jnp
from jax import lax
from jax.sharding import Mesh
from jax.sharding import PartitionSpec as P

ADAPTER_SCALING = 0.5
EPS = 1e-06
F32 = jnp.float32
BF16 = jnp.bfloat16


def contract(left, right, dims):
    return lax.dot_general(left, right, ((dims[:1], dims[1:]), ((), ())), preferred_element_type=F32)


def exchange(value, axes):
    return lax.all_to_all(value, axes, 0, 0, tiled=True)


def inverse_rms(rows):
    return lax.rsqrt(jnp.mean(rows * rows, axis=-1, keepdims=True) + EPS)


def shards(hidden_in, key_grad, key_weight, adapter_a, adapter_b, norm_gain, keep_flags, valid_counts):
    tokens, width = hidden_in.shape[1:]
    key_width = key_grad.shape[2]
    rank = adapter_a.shape[1]
    chips_y, cores = lax.axis_size("y"), lax.axis_size("core")
    nx, nz = lax.axis_size("x"), lax.axis_size("z")
    replicas = nx * nz
    half = tokens // cores
    col_share = width // replicas
    x_cols = width // nx
    scale_factor = ADAPTER_SCALING / math.sqrt(tokens * replicas)

    weight = (
        key_weight[0].astype(F32) + ADAPTER_SCALING * contract(adapter_a[0], adapter_b[0], (0, 0))
    ).astype(BF16)
    weight_z = lax.all_gather(weight, "z", axis=0, tiled=True)

    positions = lax.broadcasted_iota(jnp.int32, (tokens, 1), 0)
    live = (positions < valid_counts[0]) & (keep_flags[0] > 0)
    masked = jnp.where(live, key_grad[0], jnp.zeros_like(key_grad[0]))
    masked_x = exchange(jnp.broadcast_to(masked[None], (nx, tokens, key_width)), "x")
    masked_x = masked_x.reshape(nx, cores, half, key_width).transpose(1, 0, 2, 3)
    masked_x = masked_x.reshape(nx * tokens, key_width)

    hidden_pair = exchange(hidden_in[0].reshape(cores, half, width), "core").astype(F32)
    gain_pair = lax.all_gather(norm_gain, "core", axis=0, tiled=True)[:, None, :]
    inv_pair = inverse_rms(hidden_pair)

    resid = hidden_in[0].astype(F32)
    normed = (resid * inverse_rms(resid) * norm_gain).astype(BF16)
    lowrank = contract(masked, adapter_b[0], (1, 1)).astype(BF16)
    part_a = (scale_factor * contract(lowrank, normed, (0, 0))).astype(BF16)
    part_a = part_a.reshape(rank, replicas, col_share).transpose(1, 0, 2)

    a_z = lax.all_gather(adapter_a, "z", axis=0, tiled=True)
    a_full = lax.all_gather(a_z, "x", axis=0, tiled=True)
    a_full = a_full.transpose(1, 0, 2).reshape(rank, width)
    projected = contract(normed, a_full, (1, 1)).astype(BF16)
    part_b = (scale_factor * contract(projected, masked, (0, 0))).astype(BF16)
    part_b = part_b.reshape(rank, replicas, key_width // replicas).transpose(1, 0, 2)
    part_b = part_b.reshape(replicas, -1, col_share)
    parts = exchange(jnp.concatenate([part_a, part_b], axis=1), ("x", "z"))
    summed = jnp.sum(parts.astype(F32), axis=0)
    grad_a = summed[:rank]
    grad_b = summed[rank:].reshape(rank, key_width // replicas)

    dnorm = contract(masked_x, weight_z, (1, 1)).astype(BF16)
    dnorm = exchange(dnorm.reshape(cores * nx, half, x_cols), ("core", "x"))
    dnorm = dnorm.reshape(cores, nx, half, x_cols).transpose(0, 2, 1, 3).reshape(cores, half, width)
    slope = gain_pair * dnorm.astype(F32)
    inner = jnp.mean(hidden_pair * slope, axis=-1, keepdims=True)
    term = (inv_pair * (slope - hidden_pair * inv_pair * inv_pair * inner)).astype(BF16)

    upper, lower = term[1].astype(F32), term[0].astype(F32)
    total = (upper + lower).astype(BF16)
    slices = exchange(total.reshape(chips_y, half // chips_y, width), "y").astype(F32)
    running = jnp.zeros_like(slices[0])
    above = [None] * chips_y
    for chip in reversed(range(chips_y)):
        above[chip] = running.astype(BF16)
        running = running + slices[chip]
    above = exchange(jnp.stack(above), "y").reshape(half, width).astype(F32)
    stream_upper = (above + upper).astype(BF16)
    stream_lower = (stream_upper.astype(F32) + lower).astype(BF16)
    stream = exchange(jnp.stack([stream_lower, stream_upper]), "core").reshape(tokens, width)
    return stream[None], grad_a[None], grad_b[None]


def solution(mesh):
    sections, replicas = mesh.devices.shape
    split = Mesh(mesh.devices.reshape(sections // 2, 2, 4, replicas // 4), ("y", "core", "x", "z"))
    section, dp = ("y", "core"), ("x", "z")
    return jax.shard_map(
        shards,
        mesh=split,
        in_specs=(
            P(section, dp, None),
            P(section, dp, None),
            P(section, dp, None),
            P(section, None, dp),
            P(section, None, None),
            P(section, None),
            P(section),
            P(dp),
        ),
        out_specs=(P(section, dp, None), P(section, None, dp), P(section, None, dp)),
        check_vma=False,
    )
```

```python
import functools
import math

import jax
import jax.numpy as jnp
from jax import lax
from jax.experimental import pallas as pl
from jax.experimental.pallas import tpu as pltpu
from jax.sharding import Mesh
from jax.sharding import PartitionSpec as P

ADAPTER_SCALING = 0.5
EPS = 1e-06
F32 = jnp.float32
BF16 = jnp.bfloat16
SMEM = pl.BlockSpec(memory_space=pltpu.SMEM)
ANY = pl.BlockSpec(memory_space=pl.ANY)
HBM = pl.BlockSpec(memory_space=pltpu.HBM)


def contract(left, right, dims):
    return lax.dot_general(left, right, ((dims[:1], dims[1:]), ((), ())), preferred_element_type=F32)


def exchange(value, axes):
    return lax.all_to_all(value, axes, 0, 0, tiled=True)


def shift(value, axis, by):
    size = lax.axis_size(axis)
    return lax.ppermute(value, axis, [(i, (i + by) % size) for i in range(size)])


def swap(value, axis, bit):
    return lax.ppermute(value, axis, [(i, i ^ bit) for i in range(lax.axis_size(axis))])


def params(megabytes=12):
    return pltpu.CompilerParams(vmem_limit_bytes=megabytes << 20)


def cost(flops, elements):
    return pl.CostEstimate(flops=flops, bytes_accessed=2 * elements, transcendentals=0)


def in_hbm(value):
    return pltpu.with_memory_space_constraint(value, pltpu.HBM)


def whole(*shape):
    return pl.BlockSpec(shape, lambda *_: (0,) * len(shape))


def fold_kernel(weight_ref, a_ref, b_ref, out_ref):
    rows = weight_ref.shape[0]
    rank, share = a_ref.shape
    low = contract(a_ref[...], b_ref[...], (0, 0))
    out_ref[:rows] = (weight_ref[...].astype(F32) + ADAPTER_SCALING * low).astype(BF16)
    groups = out_ref.shape[1] // share
    depth = rank // groups
    for group in range(groups):
        out_ref[rows:, group * share : (group + 1) * share] = a_ref[group * depth : (group + 1) * depth]


def fold(weight, a_cols, b_mat):
    rows, key_width = weight.shape
    packed = a_cols.size // key_width
    return pl.pallas_call(
        fold_kernel,
        grid=(1,),
        out_shape=jax.ShapeDtypeStruct((rows + packed, key_width), BF16),
        in_specs=[whole(*weight.shape), whole(*a_cols.shape), whole(*b_mat.shape)],
        out_specs=whole(rows + packed, key_width),
        compiler_params=params(),
        cost_estimate=cost(2 * a_cols.shape[0] * weight.size, 3 * weight.size),
        name="fold",
    )(weight, a_cols, b_mat)


def mask_kernel(keep_ref, count_ref, grad_ref, *refs):
    out_ref = refs[-1]
    grad = grad_ref[...]
    positions = lax.broadcasted_iota(jnp.int32, (grad.shape[0], 1), 0)
    limit = jnp.where(keep_ref[0] > 0, count_ref[0], 0)
    out_ref[0] = jnp.where(positions < limit, grad, jnp.zeros_like(grad))


def mask(keep, count, grad, after, copies):
    return pl.pallas_call(
        mask_kernel,
        grid=(copies,),
        out_shape=pltpu.HBM((copies,) + grad.shape, BF16),
        in_specs=[SMEM, SMEM, whole(*grad.shape)] + [ANY] * len(after),
        out_specs=pl.BlockSpec((1,) + grad.shape, lambda i: (i, 0, 0)),
        compiler_params=params(),
        cost_estimate=cost(grad.size, 5 * grad.size),
        name="mask",
    )(keep, count, grad, *after)


def products_kernel(share, count, given, masked_ref, *refs):
    blocks, (out_ref, a_ref) = refs[:count], refs[-2:]
    nx, tokens, key_width = masked_ref.shape
    half = out_ref.shape[1]
    rows = masked_ref[...].reshape(nx * tokens, key_width)
    at = 0
    for block in blocks:
        depth = min(block.shape[0], share)
        columns = contract(rows, block[:depth], (1, 1)).astype(BF16)
        for chip in range(nx):
            for part in range(tokens // half):
                start = chip * tokens + part * half
                out_ref[part * nx + chip, :, at : at + depth] = columns[start : start + half]
        at += depth
    slot = 0
    for ref in refs[count : count + given]:
        a_ref[slot : slot + ref.shape[0]] = ref[...]
        slot += ref.shape[0]
    for block in blocks:
        if block.shape[0] > share:
            a_ref[slot] = block[share:]
            slot += 1


def products(masked_x, blocks, share, cores, width, a_parts=(), column=0, into=None, after=()):
    nx, tokens, key_width = masked_x.shape
    columns = sum(min(block.shape[0], share) for block in blocks)
    shape = (cores * nx, tokens // cores, width)
    extra = list(after) + ([] if into is None else [into])
    slots = sum(part.shape[0] for part in a_parts) + sum(block.shape[0] > share for block in blocks)
    rows = max(block.shape[0] for block in blocks) - share
    return pl.pallas_call(
        functools.partial(products_kernel, share, len(blocks), len(a_parts)),
        grid=(1,),
        out_shape=(pltpu.HBM(shape, BF16), jax.ShapeDtypeStruct((slots, rows, key_width), BF16)),
        in_specs=[whole(*masked_x.shape)]
        + [whole(*value.shape) for value in (*blocks, *a_parts)]
        + [ANY] * len(after)
        + [HBM] * (into is not None),
        out_specs=(
            pl.BlockSpec(shape[:2] + (columns,), lambda i: (0, 0, column // columns)),
            whole(slots, rows, key_width),
        ),
        input_output_aliases={} if into is None else {len(blocks) + len(a_parts) + len(extra): 0},
        compiler_params=params(20),
        cost_estimate=cost(2 * masked_x.size * columns, 2 * masked_x.size),
        name="products",
    )(masked_x, *blocks, *a_parts, *extra)


def term_kernel(share, offsets, nz, place_ref, own_ref, other_ref, gain_ref, *refs):
    pieces, (term_ref, total_ref) = refs[: len(offsets)], refs[-2:]
    rows, width = own_ref.shape
    nx = pieces[0].shape[0] // 2
    z, core = place_ref[0], place_ref[1]

    def places():
        for chip in range(nx):
            for piece, piece_offsets in zip(pieces, offsets):
                for at, offset in enumerate(piece_offsets):
                    slot = lax.rem(z + (offset + nz), nz)
                    start = pl.multiple_of(chip * (nz * share) + slot * share, share)
                    yield chip, piece, slice(at * share, (at + 1) * share), pl.ds(start, share)

    layers = ((own_ref, core), (other_ref, 1 - core))
    factors = []
    for hidden_ref, layer in layers:
        partial = jnp.zeros((rows, share), F32)
        squares = jnp.zeros((rows, share), F32)
        for chip, piece, cols, place in places():
            slope = gain_ref[layer, :, place] * piece[layer * nx + chip, :, cols].astype(F32)
            hidden = hidden_ref[:, place].astype(F32)
            partial += hidden * slope
            squares += hidden * hidden
        inv = lax.rsqrt(jnp.sum(squares, axis=1, keepdims=True) * (1.0 / width) + EPS)
        inner = jnp.sum(partial, axis=1, keepdims=True) * (1.0 / width)
        factors.append((inv, inv * inv * inner))
    for chip, piece, cols, place in places():
        total = None
        for (hidden_ref, layer), (inv, factor) in zip(layers, factors):
            slope = gain_ref[layer, :, place] * piece[layer * nx + chip, :, cols].astype(F32)
            term = (inv * (slope - hidden_ref[:, place].astype(F32) * factor)).astype(BF16)
            term_ref[layer, :, place] = term
            total = term.astype(F32) if total is None else total + term.astype(F32)
        total_ref[:, place] = total.astype(BF16)


def norm_backward(place, hidden, other, gain_pair, pieces, offsets, after, share, nz):
    half, width = other.shape[0] // 2, other.shape[1]
    rows = 16
    steps = half // rows

    def by_rows(array):
        return pl.BlockSpec((array.shape[0], rows, array.shape[2]), lambda i, at: (0, i, 0))

    half_block = pl.BlockSpec((rows, width), lambda i, at: (at[1] * steps + i, 0))
    return pl.pallas_call(
        functools.partial(term_kernel, share, offsets, nz),
        grid_spec=pltpu.PrefetchScalarGridSpec(
            num_scalar_prefetch=1,
            grid=(steps,),
            in_specs=[
                half_block,
                half_block,
                whole(*gain_pair.shape),
            ]
            + [by_rows(piece) for piece in pieces]
            + [ANY] * len(after),
            out_specs=(pl.BlockSpec((2, rows, width), lambda i, at: (0, i, 0)), pl.BlockSpec((rows, width), lambda i, at: (i, 0))),
        ),
        out_shape=(pltpu.HBM((2, half, width), BF16), pltpu.HBM((half, width), BF16)),
        compiler_params=params(),
        cost_estimate=cost(20 * hidden.size, 4 * hidden.size),
        name="norm_backward",
    )(place, hidden, other, gain_pair, *pieces, *after)


def above_kernel(slices_ref, *refs):
    above_ref = refs[-1]
    chips = slices_ref.shape[0]
    running = jnp.zeros(slices_ref.shape[1:], F32)
    for chip in reversed(range(chips)):
        above_ref[chip] = running.astype(BF16)
        if chip:
            running += slices_ref[chip].astype(F32)


def sums_above(slices, after):
    chips, rows, width = slices.shape
    spec = pl.BlockSpec((chips, rows, width // 2), lambda i: (0, 0, i))
    return pl.pallas_call(
        above_kernel,
        grid=(2,),
        out_shape=pltpu.HBM(slices.shape, BF16),
        in_specs=[spec] + [ANY] * len(after),
        out_specs=spec,
        compiler_params=params(),
        cost_estimate=cost(slices.size, 2 * slices.size),
        name="sums_above",
    )(slices, *after)


def normalise_kernel(share, hidden_ref, gain_ref, out_ref):
    tokens, width = hidden_ref.shape
    squares = jnp.zeros((tokens, share), F32)
    for at in range(0, width, share):
        hidden = hidden_ref[:, at : at + share].astype(F32)
        squares += hidden * hidden
    inv = lax.rsqrt(jnp.sum(squares, axis=1, keepdims=True) * (1.0 / width) + EPS)
    for at in range(0, width, share):
        cols = slice(at, at + share)
        chip, place = divmod(at, out_ref.shape[2])
        normed = hidden_ref[:, cols].astype(F32) * inv * gain_ref[:, cols]
        out_ref[chip, :, place : place + share] = normed.astype(BF16)


def normalise(hidden, gain, share, nx):
    tokens, width = hidden.shape
    rows = 64
    return pl.pallas_call(
        functools.partial(normalise_kernel, share),
        grid=(tokens // rows,),
        out_shape=pltpu.HBM((nx, tokens, width // nx), BF16),
        in_specs=[pl.BlockSpec((rows, width), lambda i: (i, 0)), whole(*gain.shape)],
        out_specs=pl.BlockSpec((nx, rows, width // nx), lambda i: (0, i, 0)),
        compiler_params=params(),
        cost_estimate=cost(6 * hidden.size, 2 * hidden.size),
        name="normalise",
    )(hidden, gain)


def partials_kernel(share, offsets, nz, scale_factor, z_ref, masked_ref, normed_ref, a_ref, b_ref, *refs):
    part_ref, projected_ref = refs[-2:]
    nx, tokens, key_width = masked_ref.shape
    lowrank = contract(masked_ref[...].reshape(nx * tokens, key_width), b_ref[...], (1, 1)).astype(BF16)
    for at in range(nz):
        normed = normed_ref[:, :, at * share : (at + 1) * share].reshape(nx * tokens, share)
        part_ref[at] = (scale_factor * contract(lowrank, normed, (0, 0))).astype(BF16)
    total = jnp.zeros(projected_ref.shape, F32)
    for at, offset in enumerate(offsets):
        slot = lax.rem(z_ref[0] + (offset + nz), nz)
        place = pl.ds(pl.multiple_of(slot * share, share), share)
        packed = a_ref[at]
        groups = packed.shape[1] // share
        a_cols = jnp.concatenate([packed[:, g * share : (g + 1) * share] for g in range(groups)], axis=0)
        total += contract(a_cols, normed_ref[:, :, place].reshape(nx * tokens, share), (1, 1))
    projected_ref[...] = total.astype(BF16)


def partials(z, masked_x, normed_x, a_own, b_mat, offsets, after, share, nz, scale_factor):
    nx, tokens, _ = masked_x.shape
    rank = b_mat.shape[0]
    operands = (masked_x, normed_x, a_own, b_mat)
    shapes = ((nz, rank, share), (rank, nx * tokens))
    return pl.pallas_call(
        functools.partial(partials_kernel, share, offsets, nz, scale_factor),
        grid=(1,),
        out_shape=tuple(jax.ShapeDtypeStruct(shape, BF16) for shape in shapes),
        in_specs=[SMEM] + [whole(*operand.shape) for operand in operands] + [HBM] * len(after),
        out_specs=tuple(whole(*shape) for shape in shapes),
        compiler_params=params(16),
        cost_estimate=cost(4 * normed_x.size * rank, 2 * normed_x.size),
        name="partials",
    )(z, *operands, *after)


def partial_b_kernel(scale_factor, x_ref, masked_ref, *refs):
    parts, out_ref = refs[:-1], refs[-1]
    nx, tokens, _ = masked_ref.shape
    share = out_ref.shape[1]
    projected = parts[0][...].astype(F32)
    for part in parts[1:]:
        projected += part[...].astype(F32)
    place = pl.ds(pl.multiple_of(x_ref[0] * share, share), share)
    rows = masked_ref[:, :, place].reshape(nx * tokens, share)
    out_ref[...] = (scale_factor * contract(projected.astype(BF16), rows, (1, 0))).astype(BF16)


def partial_b(x, masked_x, parts, scale_factor):
    nx, _, key_width = masked_x.shape
    shape = (parts[0].shape[0], key_width // nx)
    return pl.pallas_call(
        functools.partial(partial_b_kernel, scale_factor),
        grid=(1,),
        out_shape=jax.ShapeDtypeStruct(shape, BF16),
        in_specs=[SMEM, whole(*masked_x.shape)] + [whole(*part.shape) for part in parts],
        out_specs=whole(*shape),
        compiler_params=params(),
        cost_estimate=cost(2 * masked_x.size * shape[0] // nx, masked_x.size),
        name="partial_b",
    )(x, masked_x, *parts)


def halves_kernel(side_ref, a_ref, b_ref, *refs):
    kept_ref, sent_ref = refs[-2:]
    half = kept_ref.shape[0]
    rank = a_ref.shape[1]
    for at in range(half):
        for out, begin in ((kept_ref, side_ref[0] * half), (sent_ref, (1 - side_ref[0]) * half)):
            out[at, :rank] = a_ref[begin + at]
            out[at, rank:] = b_ref[begin + at]


def halves(part_a, part_b, side, after):
    nz, rank, share = part_a.shape
    shape = (nz // 2, rank + part_b.shape[1], share)
    return pl.pallas_call(
        halves_kernel,
        grid=(1,),
        out_shape=(jax.ShapeDtypeStruct(shape, BF16),) * 2,
        in_specs=[SMEM, whole(*part_a.shape), whole(*part_b.shape)] + [HBM] * len(after),
        out_specs=(whole(*shape),) * 2,
        compiler_params=params(),
        cost_estimate=cost(0, 2 * part_a.size),
        name="halves",
    )(side, part_a, part_b, *after)


def add_kernel(count, side_ref, *refs):
    outs = refs[-1:] if refs[0].shape[0] == 1 else refs[-2:]
    half = outs[0].shape[0]
    for at in range(half):
        for out, begin in zip(outs, (side_ref[0] * half, (1 - side_ref[0]) * half)):
            where = begin + at if len(outs) == 2 else at
            total = refs[0][where].astype(F32)
            for ref in refs[1:count]:
                total += ref[where].astype(F32)
            out[at] = total.astype(out.dtype)


def add(values, side):
    shape = values[0].shape
    single = shape[0] == 1
    half = shape if single else (shape[0] // 2,) + shape[1:]
    out = jax.ShapeDtypeStruct(half, F32 if single else BF16)
    return pl.pallas_call(
        functools.partial(add_kernel, len(values)),
        grid=(1,),
        out_shape=(out,) * (1 if single else 2),
        in_specs=[SMEM] + [whole(*shape)] * len(values),
        out_specs=(whole(*half),) * (1 if single else 2),
        compiler_params=params(),
        cost_estimate=cost(len(values) * values[0].size, 4 * values[0].size),
        name="add",
    )(side, *values)


def scatter_sum(part_a, part_b, axis, after=()):
    bit = lax.axis_size(axis) // 2
    index = lax.axis_index(axis)
    kept, sent = halves(part_a, part_b, ((index // bit) % 2)[None], after)
    while bit > 1:
        received = swap(sent, axis, bit)
        bit //= 2
        kept, sent = add([kept, received], ((index // bit) % 2)[None])
    return add([kept, swap(sent, axis, bit)], index[None])[0][0]


def shards(hidden_in, key_grad, key_weight, adapter_a, adapter_b, norm_gain, keep_flags, valid_counts):
    tokens, width = hidden_in.shape[1:]
    key_width = key_grad.shape[2]
    rank = adapter_a.shape[1]
    chips_y, cores = lax.axis_size("y"), lax.axis_size("core")
    nx, nz = lax.axis_size("x"), lax.axis_size("z")
    replicas = nx * nz
    half = tokens // cores
    share = width // replicas
    scale_factor = ADAPTER_SCALING / math.sqrt(tokens * replicas)
    x_index, z_index, core = (lax.axis_index(axis) for axis in ("x", "z", "core"))

    block = fold(in_hbm(key_weight[0]), in_hbm(adapter_a[0]), in_hbm(adapter_b[0]))
    masked = mask(keep_flags, valid_counts, in_hbm(key_grad[0]), [block], nx)
    masked_x = exchange(masked, "x")
    up, down = [block], [block]
    for step in range(1, nz // 2):
        up.append(shift(up[-1], "z", 1))
        down.append(shift(down[-1], "z", -1))
    up.append(shift(up[-1], "z", 1))

    hidden = in_hbm(hidden_in[0])
    other = in_hbm(swap(hidden, "core", 1))
    gain_pair = lax.all_gather(norm_gain, "core", axis=0, tiled=True)[:, None, :]

    rounds = [
        ([block, up[1], down[1]], [0, -1, 1], 0),
        ([up[2], down[2]], [-2, 2], 4),
        ([up[3], down[3]], [-3, 3], 6),
        ([up[4]], [-4], 3),
    ]
    normed_x = exchange(normalise(hidden, norm_gain, share, nx), "x")
    dnorm, a_own = None, None
    for blocks, _, slot in rounds:
        dnorm, a_own = products(
            masked_x,
            blocks,
            share,
            cores,
            nz * share,
            [] if a_own is None else [a_own],
            column=slot * share,
            into=dnorm,
            after=[normed_x] if slot == 6 else [],
        )
    a_offsets = [offset for _, round_offsets, _ in rounds for offset in round_offsets]
    offsets = [0, -1, 1, -4, -2, 2, -3, 3]
    dnorm = in_hbm(dnorm)
    piece = in_hbm(exchange(dnorm, ("core", "x")))

    part_a, projected = partials(
        z_index[None], masked_x, normed_x, a_own, adapter_b[0], a_offsets, [dnorm], share, nz, scale_factor
    )
    projected = [projected] + [shift(projected, "x", by) for by in (-1, 1, 2)]
    part_b = partial_b(x_index[None], masked_x, projected, scale_factor)
    part_b = part_b.reshape(rank, nz, key_width // replicas).transpose(1, 0, 2).reshape(nz, -1, share)
    term, total = norm_backward(
        jnp.stack([z_index, core]), hidden, other, gain_pair, [piece], [offsets], [part_a], share, nz
    )

    slices = exchange(total.reshape(chips_y, half // chips_y, width), "y")
    above_slices = sums_above(slices, [part_b])
    above = exchange(above_slices, "y").reshape(half, width).astype(F32)
    stream_upper = (above + term[1].astype(F32)).astype(BF16)
    stream_lower = (stream_upper.astype(F32) + term[0].astype(F32)).astype(BF16)
    stream = exchange(jnp.stack([stream_lower, stream_upper]), "core").reshape(tokens, width)
    summed = scatter_sum(part_a, part_b, "z", [above_slices])
    grad_a = summed[:rank]
    grad_b = summed[rank:].reshape(rank, key_width // replicas)
    return stream[None], grad_a[None], grad_b[None]


def solution(mesh):
    sections, replicas = mesh.devices.shape
    split = Mesh(mesh.devices.reshape(sections // 2, 2, 4, replicas // 4), ("y", "core", "x", "z"))
    section, dp = ("y", "core"), ("x", "z")
    return jax.shard_map(
        shards,
        mesh=split,
        in_specs=(
            P(section, dp, None),
            P(section, dp, None),
            P(section, dp, None),
            P(section, None, dp),
            P(section, None, None),
            P(section, None),
            P(section),
            P(dp),
        ),
        out_specs=(P(section, dp, None), P(section, None, dp), P(section, None, dp)),
        check_vma=False,
    )
```

```python
import functools
import math

import jax
import jax.numpy as jnp
from jax import lax
from jax.experimental import pallas as pl
from jax.experimental.pallas import tpu as pltpu
from jax.sharding import Mesh
from jax.sharding import PartitionSpec as P

ADAPTER_SCALING = 0.5
EPS = 1e-06
F32 = jnp.float32
BF16 = jnp.bfloat16
SMEM = pl.BlockSpec(memory_space=pltpu.SMEM)
ANY = pl.BlockSpec(memory_space=pl.ANY)
VMEM = pl.BlockSpec(memory_space=pltpu.VMEM)
HBM = pl.BlockSpec(memory_space=pltpu.HBM)


def contract(left, right, dims):
    return lax.dot_general(left, right, ((dims[:1], dims[1:]), ((), ())), preferred_element_type=F32)


def exchange(value, axes):
    return lax.all_to_all(value, axes, 0, 0, tiled=True)


def shift(value, axis, by):
    size = lax.axis_size(axis)
    return lax.ppermute(value, axis, [(i, (i + by) % size) for i in range(size)])


def swap(value, axis, bit):
    return lax.ppermute(value, axis, [(i, i ^ bit) for i in range(lax.axis_size(axis))])


def params(megabytes=12):
    return pltpu.CompilerParams(vmem_limit_bytes=megabytes << 20)


def cost(flops, elements):
    return pl.CostEstimate(flops=flops, bytes_accessed=2 * elements, transcendentals=0)


def in_hbm(value):
    return pltpu.with_memory_space_constraint(value, pltpu.HBM)


def whole(*shape):
    return pl.BlockSpec(shape, lambda *_: (0,) * len(shape))


def prepare_kernel(keep_ref, count_ref, weight_ref, a_ref, b_ref, grad_ref, block_ref, masked_ref):
    grad = grad_ref[...]
    positions = lax.broadcasted_iota(jnp.int32, (grad.shape[0], 1), 0)
    live = (positions < count_ref[...]) & (keep_ref[...] > 0)
    masked = jnp.where(live, grad, jnp.zeros_like(grad))
    for copy in range(masked_ref.shape[0]):
        masked_ref[copy] = masked
    rows = weight_ref.shape[0]
    rank, share = a_ref.shape
    low = contract(a_ref[...], b_ref[...], (0, 0))
    block_ref[:rows] = (weight_ref[...].astype(F32) + ADAPTER_SCALING * low).astype(BF16)
    groups = block_ref.shape[1] // share
    depth = rank // groups
    for group in range(groups):
        block_ref[rows:, group * share : (group + 1) * share] = a_ref[group * depth : (group + 1) * depth]


def prepare(keep, count, weight, a_cols, b_mat, grad, copies):
    rows, key_width = weight.shape
    shapes = ((rows + a_cols.size // key_width, key_width), (copies,) + grad.shape)
    return pl.pallas_call(
        prepare_kernel,
        grid=(1,),
        out_shape=(jax.ShapeDtypeStruct(shapes[0], BF16), pltpu.HBM(shapes[1], BF16)),
        in_specs=[whole(*operand.shape) for operand in (keep, count, weight, a_cols, b_mat, grad)],
        out_specs=tuple(whole(*shape) for shape in shapes),
        compiler_params=params(),
        cost_estimate=cost(2 * a_cols.shape[0] * weight.size, 8 * weight.size),
        name="prepare",
    )(keep, count, weight, a_cols, b_mat, grad)


def products_kernel(share, count, masked_ref, *refs):
    blocks, (out_ref, a_ref) = refs[:count], refs[-2:]
    nx, tokens, key_width = masked_ref.shape
    half = out_ref.shape[1]
    rows = masked_ref[...].reshape(nx * tokens, key_width)
    for at, block in enumerate(blocks):
        columns = contract(rows, block[:share], (1, 1)).astype(BF16)
        for chip in range(nx):
            for part in range(tokens // half):
                start = chip * tokens + part * half
                out_ref[part * nx + chip, :, at * share : (at + 1) * share] = columns[start : start + half]
    for slot, block in enumerate(blocks):
        a_ref[slot] = block[share:]


def products(masked_x, blocks, share, cores, width, column=0, into=None, after=()):
    nx, tokens, key_width = masked_x.shape
    columns = share * len(blocks)
    shape = (cores * nx, tokens // cores, width)
    extra = list(after) + ([] if into is None else [into])
    a_shape = (len(blocks), blocks[0].shape[0] - share, key_width)
    return pl.pallas_call(
        functools.partial(products_kernel, share, len(blocks)),
        grid=(1,),
        out_shape=(pltpu.HBM(shape, BF16), pltpu.HBM(a_shape, BF16)),
        in_specs=[whole(*masked_x.shape)]
        + [whole(*value.shape) for value in blocks]
        + [ANY] * len(after)
        + [HBM] * (into is not None),
        out_specs=(
            pl.BlockSpec(shape[:2] + (columns,), lambda i: (0, 0, column // columns)),
            whole(*a_shape),
        ),
        input_output_aliases={} if into is None else {len(blocks) + len(extra): 0},
        compiler_params=params(20),
        cost_estimate=cost(2 * masked_x.size * columns, 2 * masked_x.size),
        name="products",
    )(masked_x, *blocks, *extra)


def inverse_kernel(share, rows, core_ref, own_ref, other_ref, *refs):
    out_ref = refs[-1]
    half = out_ref.shape[1]
    width = own_ref.shape[1]
    for slot, hidden_ref in enumerate((own_ref, other_ref)):
        for at in range(0, half, rows):
            span = pl.ds(pl.multiple_of(core_ref[0] * half + at, rows), rows)
            squares = jnp.zeros((rows, share), F32)
            for column in range(0, width, share):
                hidden = hidden_ref[span, column : column + share].astype(F32)
                squares += hidden * hidden
            inv = lax.rsqrt(jnp.sum(squares, axis=1, keepdims=True) * (1.0 / width) + EPS)
            out_ref[slot, at : at + rows] = jnp.broadcast_to(inv, (rows, out_ref.shape[2]))


def inverses(core, hidden, other, after, share):
    shape = (2, hidden.shape[0] // 2, 128)
    return pl.pallas_call(
        functools.partial(inverse_kernel, share, 32),
        grid=(1,),
        out_shape=jax.ShapeDtypeStruct(shape, F32),
        in_specs=[SMEM, whole(*hidden.shape), whole(*other.shape)] + [HBM] * len(after),
        out_specs=whole(*shape),
        compiler_params=params(16),
        cost_estimate=cost(3 * hidden.size, 2 * hidden.size),
        name="inverses",
    )(core, hidden, other, *after)


def term_kernel(share, offsets, place_ref, own_ref, other_ref, inv_ref, gain_ref, piece_ref, *refs):
    mine_ref, theirs_ref, total_ref = refs[-3:]
    rows, width = own_ref.shape
    nz = len(offsets)
    nx = piece_ref.shape[0] // 2
    z, core = place_ref[0], place_ref[1]
    columns = []
    for chip in range(nx):
        for at, offset in enumerate(offsets):
            slot = lax.rem(z + (offset + nz), nz)
            start = pl.multiple_of(chip * (nz * share) + slot * share, share)
            columns.append((chip, slice(at * share, (at + 1) * share), pl.ds(start, share)))

    layers = ((own_ref, core), (other_ref, 1 - core))
    factors = []
    for index, (hidden_ref, layer) in enumerate(layers):
        partial = jnp.zeros((rows, share), F32)
        for chip, cols, place in columns:
            slope = gain_ref[layer, :, place] * piece_ref[layer * nx + chip, :, cols].astype(F32)
            partial += hidden_ref[:, place].astype(F32) * slope
        inv = inv_ref[index, :, :1]
        inner = jnp.sum(partial, axis=1, keepdims=True) * (1.0 / width)
        factors.append((inv, inv * inv * inner))
    for chip, cols, place in columns:
        terms = []
        for (hidden_ref, layer), (inv, factor) in zip(layers, factors):
            slope = gain_ref[layer, :, place] * piece_ref[layer * nx + chip, :, cols].astype(F32)
            terms.append((inv * (slope - hidden_ref[:, place].astype(F32) * factor)).astype(BF16))
        total = (terms[0].astype(F32) + terms[1].astype(F32)).astype(BF16)
        total_ref[:, place] = total
        mine_ref[:, place] = jnp.where(core > 0, terms[0], total)
        theirs_ref[:, place] = jnp.where(core > 0, total, terms[1])


def norm_backward(place, hidden, other, inv_pair, gain_pair, piece, offsets, after, share):
    half, width = other.shape[0] // 2, other.shape[1]
    rows = 16
    steps = half // rows
    half_block = pl.BlockSpec((rows, width), lambda i, at: (at[1] * steps + i, 0))
    row_block = pl.BlockSpec((rows, width), lambda i, at: (i, 0))

    def by_rows(array):
        return pl.BlockSpec((array.shape[0], rows, array.shape[2]), lambda i, at: (0, i, 0))

    return pl.pallas_call(
        functools.partial(term_kernel, share, offsets),
        grid_spec=pltpu.PrefetchScalarGridSpec(
            num_scalar_prefetch=1,
            grid=(steps,),
            in_specs=[half_block, half_block, by_rows(inv_pair), whole(*gain_pair.shape), by_rows(piece)]
            + [ANY] * len(after),
            out_specs=(row_block,) * 3,
        ),
        out_shape=(pltpu.HBM((half, width), BF16),) * 3,
        compiler_params=params(16),
        cost_estimate=cost(20 * hidden.size, 4 * hidden.size),
        name="norm_backward",
    )(place, hidden, other, inv_pair, gain_pair, piece, *after)


def stream_kernel(core_ref, above_ref, sum_ref, *refs):
    refs[-1][...] = (above_ref[...].astype(F32) + sum_ref[...].astype(F32)).astype(BF16)


def stream_rows_kernel(core_ref, above_ref, sum_ref, whole_ref, out_ref):
    rows = out_ref.shape[0]
    span = pl.ds(pl.multiple_of(pl.program_id(0) * rows, rows), rows)
    out_ref[...] = (above_ref[span].astype(F32) + sum_ref[span].astype(F32)).astype(BF16)


def stream_half(core, above, within, into=None):
    half, width = above.shape
    rows = 16
    steps = half // rows
    own = into is None
    sources = [pl.BlockSpec((rows, width), lambda i, at: (i, 0)) if own else pl.BlockSpec(memory_space=pltpu.VMEM)] * 2
    return pl.pallas_call(
        stream_kernel if own else stream_rows_kernel,
        grid_spec=pltpu.PrefetchScalarGridSpec(
            num_scalar_prefetch=1,
            grid=(steps,),
            in_specs=sources + ([] if own else [HBM]),
            out_specs=pl.BlockSpec(
                (rows, width), lambda i, at: ((at[0] if own else 1 - at[0]) * steps + i, 0)
            ),
        ),
        out_shape=pltpu.HBM((2 * half, width), BF16),
        input_output_aliases={} if own else {3: 0},
        compiler_params=params(),
        cost_estimate=cost(above.size, 3 * above.size),
        name="stream_half",
    )(core, above, within, *([] if own else [into]))


def above_kernel(slices_ref, *refs):
    above_ref = refs[-1]
    chips = slices_ref.shape[0]
    running = jnp.zeros(slices_ref.shape[1:], F32)
    for chip in reversed(range(chips)):
        above_ref[chip] = running.astype(BF16)
        if chip:
            running += slices_ref[chip].astype(F32)


def sums_above(slices, after):
    chips, rows, width = slices.shape
    spec = pl.BlockSpec((chips, rows, width // 2), lambda i: (0, 0, i))
    return pl.pallas_call(
        above_kernel,
        grid=(2,),
        out_shape=pltpu.HBM(slices.shape, BF16),
        in_specs=[spec] + [ANY] * len(after),
        out_specs=spec,
        compiler_params=params(),
        cost_estimate=cost(slices.size, 2 * slices.size),
        name="sums_above",
    )(slices, *after)


def normalise_kernel(share, hidden_ref, gain_ref, out_ref):
    tokens, width = hidden_ref.shape
    squares = jnp.zeros((tokens, share), F32)
    for at in range(0, width, share):
        hidden = hidden_ref[:, at : at + share].astype(F32)
        squares += hidden * hidden
    inv = lax.rsqrt(jnp.sum(squares, axis=1, keepdims=True) * (1.0 / width) + EPS)
    for at in range(0, width, share):
        cols = slice(at, at + share)
        chip, place = divmod(at, out_ref.shape[2])
        normed = hidden_ref[:, cols].astype(F32) * inv * gain_ref[:, cols]
        out_ref[chip, :, place : place + share] = normed.astype(BF16)


def normalise(hidden, gain, share, nx):
    tokens, width = hidden.shape
    rows = 64
    return pl.pallas_call(
        functools.partial(normalise_kernel, share),
        grid=(tokens // rows,),
        out_shape=pltpu.HBM((nx, tokens, width // nx), BF16),
        in_specs=[pl.BlockSpec((rows, width), lambda i: (i, 0)), whole(*gain.shape)],
        out_specs=pl.BlockSpec((nx, rows, width // nx), lambda i: (0, i, 0)),
        compiler_params=params(),
        cost_estimate=cost(6 * hidden.size, 2 * hidden.size),
        name="normalise",
    )(hidden, gain)


def partials_kernel(share, offsets, nz, scale_factor, z_ref, masked_ref, normed_ref, b_ref, *refs):
    part_ref, projected_ref = refs[-2:]
    nx, tokens, key_width = masked_ref.shape
    lowrank = contract(masked_ref[...].reshape(nx * tokens, key_width), b_ref[...], (1, 1)).astype(BF16)
    for at in range(nz):
        normed = normed_ref[:, :, at * share : (at + 1) * share].reshape(nx * tokens, share)
        part_ref[at] = (scale_factor * contract(lowrank, normed, (0, 0))).astype(BF16)
    total = jnp.zeros(projected_ref.shape, F32)
    for ref, ref_offsets in zip(refs, offsets):
        for at, offset in enumerate(ref_offsets):
            slot = lax.rem(z_ref[0] + (offset + nz), nz)
            place = pl.ds(pl.multiple_of(slot * share, share), share)
            packed = ref[at]
            groups = packed.shape[1] // share
            a_cols = jnp.concatenate([packed[:, g * share : (g + 1) * share] for g in range(groups)], axis=0)
            total += contract(a_cols, normed_ref[:, :, place].reshape(nx * tokens, share), (1, 1))
    projected_ref[...] = total.astype(BF16)


def partials(z, masked_x, normed_x, b_mat, a_rows, offsets, after, share, nz, scale_factor):
    nx, tokens, _ = masked_x.shape
    rank = b_mat.shape[0]
    operands = (masked_x, normed_x, b_mat, *a_rows)
    shapes = ((nz, rank, share), (rank, nx * tokens))
    return pl.pallas_call(
        functools.partial(partials_kernel, share, offsets, nz, scale_factor),
        grid=(1,),
        out_shape=tuple(jax.ShapeDtypeStruct(shape, BF16) for shape in shapes),
        in_specs=[SMEM] + [whole(*operand.shape) for operand in operands] + [HBM] * len(after),
        out_specs=tuple(whole(*shape) for shape in shapes),
        compiler_params=params(16),
        cost_estimate=cost(4 * normed_x.size * rank, 2 * normed_x.size),
        name="partials",
    )(z, *operands, *after)


def partial_b_kernel(scale_factor, x_ref, masked_ref, *refs):
    parts, out_ref = refs[:-1], refs[-1]
    nx, tokens, _ = masked_ref.shape
    share = out_ref.shape[1]
    projected = parts[0][...].astype(F32)
    for part in parts[1:]:
        projected += part[...].astype(F32)
    place = pl.ds(pl.multiple_of(x_ref[0] * share, share), share)
    rows = masked_ref[:, :, place].reshape(nx * tokens, share)
    out_ref[...] = (scale_factor * contract(projected.astype(BF16), rows, (1, 0))).astype(BF16)


def partial_b(x, masked_x, parts, scale_factor):
    nx, _, key_width = masked_x.shape
    shape = (parts[0].shape[0], key_width // nx)
    return pl.pallas_call(
        functools.partial(partial_b_kernel, scale_factor),
        grid=(1,),
        out_shape=jax.ShapeDtypeStruct(shape, BF16),
        in_specs=[SMEM, whole(*masked_x.shape)] + [whole(*part.shape) for part in parts],
        out_specs=whole(*shape),
        compiler_params=params(),
        cost_estimate=cost(2 * masked_x.size * shape[0] // nx, masked_x.size),
        name="partial_b",
    )(x, masked_x, *parts)


def halves_kernel(side_ref, a_ref, b_ref, *refs):
    kept_ref, sent_ref = refs[-2:]
    half = kept_ref.shape[0]
    rank = a_ref.shape[1]
    for at in range(half):
        for out, begin in ((kept_ref, side_ref[0] * half), (sent_ref, (1 - side_ref[0]) * half)):
            out[at, :rank] = a_ref[begin + at]
            out[at, rank:] = b_ref[begin + at]


def halves(part_a, part_b, side, after):
    nz, rank, share = part_a.shape
    shape = (nz // 2, rank + part_b.shape[1], share)
    return pl.pallas_call(
        halves_kernel,
        grid=(1,),
        out_shape=(jax.ShapeDtypeStruct(shape, BF16),) * 2,
        in_specs=[SMEM, whole(*part_a.shape), whole(*part_b.shape)] + [HBM] * len(after),
        out_specs=(whole(*shape),) * 2,
        compiler_params=params(),
        cost_estimate=cost(0, 2 * part_a.size),
        name="halves",
    )(side, part_a, part_b, *after)


def add_kernel(count, side_ref, *refs):
    outs = refs[-1:] if refs[0].shape[0] == 1 else refs[-2:]
    half = outs[0].shape[0]
    for at in range(half):
        for out, begin in zip(outs, (side_ref[0] * half, (1 - side_ref[0]) * half)):
            where = begin + at if len(outs) == 2 else at
            total = refs[0][where].astype(F32)
            for ref in refs[1:count]:
                total += ref[where].astype(F32)
            out[at] = total.astype(out.dtype)


def add(values, side):
    shape = values[0].shape
    single = shape[0] == 1
    half = shape if single else (shape[0] // 2,) + shape[1:]
    out = jax.ShapeDtypeStruct(half, F32 if single else BF16)
    return pl.pallas_call(
        functools.partial(add_kernel, len(values)),
        grid=(1,),
        out_shape=(out,) * (1 if single else 2),
        in_specs=[SMEM] + [whole(*shape)] * len(values),
        out_specs=(whole(*half),) * (1 if single else 2),
        compiler_params=params(),
        cost_estimate=cost(len(values) * values[0].size, 4 * values[0].size),
        name="add",
    )(side, *values)


def scatter_begin(part_a, part_b, axis):
    bit = lax.axis_size(axis) // 2
    index = lax.axis_index(axis)
    kept, sent = halves(part_a, part_b, ((index // bit) % 2)[None], [])
    return add([kept, swap(sent, axis, bit)], ((index // (bit // 2)) % 2)[None])


def scatter_end(kept, sent, axis):
    bit = lax.axis_size(axis) // 4
    index = lax.axis_index(axis)
    while bit > 1:
        received = swap(sent, axis, bit)
        bit //= 2
        kept, sent = add([kept, received], ((index // bit) % 2)[None])
    return add([kept, swap(sent, axis, bit)], index[None])[0][0]


def shards(hidden_in, key_grad, key_weight, adapter_a, adapter_b, norm_gain, keep_flags, valid_counts):
    tokens, width = hidden_in.shape[1:]
    key_width = key_grad.shape[2]
    rank = adapter_a.shape[1]
    chips_y, cores = lax.axis_size("y"), lax.axis_size("core")
    nx, nz = lax.axis_size("x"), lax.axis_size("z")
    replicas = nx * nz
    half = tokens // cores
    share = width // replicas
    scale_factor = ADAPTER_SCALING / math.sqrt(tokens * replicas)
    x_index, z_index, core = (lax.axis_index(axis) for axis in ("x", "z", "core"))

    b_mat = in_hbm(adapter_b[0])
    block, masked = prepare(
        keep_flags[None], valid_counts[None], in_hbm(key_weight[0]), in_hbm(adapter_a[0]), b_mat, in_hbm(key_grad[0]), nx
    )
    masked_x = exchange(masked, "x")
    up, down = [block], [block]
    for step in range(1, nz // 2):
        up.append(shift(up[-1], "z", 1))
        down.append(shift(down[-1], "z", -1))
    up.append(shift(up[-1], "z", 1))

    hidden = in_hbm(hidden_in[0])
    other = swap(hidden, "core", 1)
    gain_pair = lax.all_gather(norm_gain, "core", axis=0, tiled=True)[:, None, :]

    rounds = [
        ([block, up[1], down[1]], [0, -1, 1], 0),
        ([up[2], down[2]], [-2, 2], 4),
        ([up[3], down[3]], [-3, 3], 6),
        ([up[4]], [-4], 3),
    ]
    normed_x = exchange(normalise(hidden, norm_gain, share, nx), "x")
    dnorm, a_rows = None, []
    for blocks, _, slot in rounds:
        dnorm, rows = products(
            masked_x,
            blocks,
            share,
            cores,
            nz * share,
            column=slot * share,
            into=dnorm,
            after=[normed_x] if slot == 6 else [],
        )
        a_rows.append(rows)
    a_offsets = [round_offsets for _, round_offsets, _ in rounds]
    offsets = [0, -1, 1, -4, -2, 2, -3, 3]
    dnorm = in_hbm(dnorm)
    piece = exchange(dnorm, ("core", "x"))

    part_a, projected = partials(
        z_index[None], masked_x, normed_x, b_mat, a_rows, a_offsets, [dnorm], share, nz, scale_factor
    )
    projected = [projected] + [shift(projected, "x", by) for by in (-1, 1, 2)]
    part_b = partial_b(x_index[None], masked_x, projected, scale_factor)
    part_b = part_b.reshape(rank, nz, key_width // replicas).transpose(1, 0, 2).reshape(nz, -1, share)
    inv_pair = inverses(core[None], hidden, other, [dnorm], share)
    mine, theirs, total = norm_backward(
        jnp.stack([z_index, core]), hidden, other, inv_pair, gain_pair, piece, offsets, [part_a], share
    )

    slices = exchange(total.reshape(chips_y, half // chips_y, width), "y")
    kept, sent = scatter_begin(part_a, part_b, "z")
    above_slices = sums_above(slices, [kept])
    beyond = swap(theirs, "core", 1)
    above = exchange(above_slices, "y").reshape(half, width)
    summed = scatter_end(kept, sent, "z")
    above, summed = lax.optimization_barrier((above, summed))
    received = swap(above, "core", 1)
    stream = stream_half(core[None], received, beyond, stream_half(core[None], above, mine))
    grad_a = summed[:rank]
    grad_b = summed[rank:].reshape(rank, key_width // replicas)
    return stream[None], grad_a[None], grad_b[None]


def solution(mesh):
    sections, replicas = mesh.devices.shape
    split = Mesh(mesh.devices.reshape(sections // 2, 2, 4, replicas // 4), ("y", "core", "x", "z"))
    section, dp = ("y", "core"), ("x", "z")
    return jax.shard_map(
        shards,
        mesh=split,
        in_specs=(
            P(section, dp, None),
            P(section, dp, None),
            P(section, dp, None),
            P(section, None, dp),
            P(section, None, None),
            P(section, None),
            P(section),
            P(dp),
        ),
        out_specs=(P(section, dp, None), P(section, None, dp), P(section, None, dp)),
        check_vma=False,
    )
```

```python
import functools
import math

import jax
import jax.numpy as jnp
from jax import lax
from jax.experimental import pallas as pl
from jax.experimental.pallas import tpu as pltpu
from jax.sharding import Mesh
from jax.sharding import PartitionSpec as P

ADAPTER_SCALING = 0.5
EPS = 1e-06
F32 = jnp.float32
BF16 = jnp.bfloat16
SMEM = pl.BlockSpec(memory_space=pltpu.SMEM)
ANY = pl.BlockSpec(memory_space=pl.ANY)
VMEM = pl.BlockSpec(memory_space=pltpu.VMEM)
HBM = pl.BlockSpec(memory_space=pltpu.HBM)


def contract(left, right, dims):
    return lax.dot_general(left, right, ((dims[:1], dims[1:]), ((), ())), preferred_element_type=F32)


def exchange(value, axes):
    return lax.all_to_all(value, axes, 0, 0, tiled=True)


def shift(value, axis, by):
    size = lax.axis_size(axis)
    return lax.ppermute(value, axis, [(i, (i + by) % size) for i in range(size)])


def swap(value, axis, bit):
    return lax.ppermute(value, axis, [(i, i ^ bit) for i in range(lax.axis_size(axis))])


def params(megabytes=12):
    return pltpu.CompilerParams(vmem_limit_bytes=megabytes << 20)


def cost(flops, elements):
    return pl.CostEstimate(flops=flops, bytes_accessed=2 * elements, transcendentals=0)


def in_hbm(value):
    return pltpu.with_memory_space_constraint(value, pltpu.HBM)


def whole(*shape):
    return pl.BlockSpec(shape, lambda *_: (0,) * len(shape))


def prepare_kernel(keep_ref, count_ref, weight_ref, a_ref, b_ref, grad_ref, block_ref, masked_ref):
    grad = grad_ref[...]
    positions = lax.broadcasted_iota(jnp.int32, (grad.shape[0], 1), 0)
    live = (positions < count_ref[...]) & (keep_ref[...] > 0)
    masked = jnp.where(live, grad, jnp.zeros_like(grad))
    for copy in range(masked_ref.shape[0]):
        masked_ref[copy] = masked
    rows = weight_ref.shape[0]
    rank, share = a_ref.shape
    low = contract(a_ref[...], b_ref[...], (0, 0))
    block_ref[:rows] = (weight_ref[...].astype(F32) + ADAPTER_SCALING * low).astype(BF16)
    groups = block_ref.shape[1] // share
    depth = rank // groups
    for group in range(groups):
        block_ref[rows:, group * share : (group + 1) * share] = a_ref[group * depth : (group + 1) * depth]


def prepare(keep, count, weight, a_cols, b_mat, grad, copies):
    rows, key_width = weight.shape
    shapes = ((rows + a_cols.size // key_width, key_width), (copies,) + grad.shape)
    return pl.pallas_call(
        prepare_kernel,
        grid=(1,),
        out_shape=(jax.ShapeDtypeStruct(shapes[0], BF16), pltpu.HBM(shapes[1], BF16)),
        in_specs=[whole(*operand.shape) for operand in (keep, count, weight, a_cols, b_mat, grad)],
        out_specs=tuple(whole(*shape) for shape in shapes),
        compiler_params=params(),
        cost_estimate=cost(2 * a_cols.shape[0] * weight.size, 8 * weight.size),
        name="prepare",
    )(keep, count, weight, a_cols, b_mat, grad)


def products_kernel(share, count, masked_ref, *refs):
    blocks, (out_ref, a_ref) = refs[:count], refs[-2:]
    nx, tokens, key_width = masked_ref.shape
    half = out_ref.shape[2]
    rows = masked_ref[...].reshape(nx * tokens, key_width)
    for at, block in enumerate(blocks):
        columns = contract(rows, block[:share], (1, 1)).astype(BF16)
        for chip in range(nx):
            for part in range(tokens // half):
                start = chip * tokens + part * half
                out_ref[part * nx + chip, at] = columns[start : start + half]
    for slot, block in enumerate(blocks):
        a_ref[slot] = block[share:]


def products(masked_x, blocks, share, cores, slots, slot=0, into=None, after=()):
    nx, tokens, key_width = masked_x.shape
    count = len(blocks)
    shape = (cores * nx, slots, tokens // cores, share)
    extra = list(after) + ([] if into is None else [into])
    a_shape = (len(blocks), blocks[0].shape[0] - share, key_width)
    return pl.pallas_call(
        functools.partial(products_kernel, share, len(blocks)),
        grid=(1,),
        out_shape=(pltpu.HBM(shape, BF16), pltpu.HBM(a_shape, BF16)),
        in_specs=[whole(*masked_x.shape)]
        + [whole(*value.shape) for value in blocks]
        + [ANY] * len(after)
        + [HBM] * (into is not None),
        out_specs=(
            pl.BlockSpec((shape[0], count) + shape[2:], lambda i: (0, slot // count, 0, 0)),
            whole(*a_shape),
        ),
        input_output_aliases={} if into is None else {len(blocks) + len(extra): 0},
        compiler_params=params(20),
        cost_estimate=cost(2 * masked_x.size * share * count, 2 * masked_x.size),
        name="products",
    )(masked_x, *blocks, *extra)


def inverse_kernel(share, rows, core_ref, own_ref, other_ref, *refs):
    out_ref = refs[-1]
    half = out_ref.shape[1]
    width = own_ref.shape[1]
    for slot, hidden_ref in enumerate((own_ref, other_ref)):
        for at in range(0, half, rows):
            span = pl.ds(pl.multiple_of(core_ref[0] * half + at, rows), rows)
            squares = jnp.zeros((rows, share), F32)
            for column in range(0, width, share):
                hidden = hidden_ref[span, column : column + share].astype(F32)
                squares += hidden * hidden
            inv = lax.rsqrt(jnp.sum(squares, axis=1, keepdims=True) * (1.0 / width) + EPS)
            out_ref[slot, at : at + rows] = jnp.broadcast_to(inv, (rows, out_ref.shape[2]))


def inverses(core, hidden, other, after, share):
    shape = (2, hidden.shape[0] // 2, 128)
    return pl.pallas_call(
        functools.partial(inverse_kernel, share, 32),
        grid=(1,),
        out_shape=jax.ShapeDtypeStruct(shape, F32),
        in_specs=[SMEM, whole(*hidden.shape), whole(*other.shape)] + [HBM] * len(after),
        out_specs=whole(*shape),
        compiler_params=params(16),
        cost_estimate=cost(3 * hidden.size, 2 * hidden.size),
        name="inverses",
    )(core, hidden, other, *after)


def term_kernel(share, offsets, place_ref, own_ref, other_ref, inv_ref, gain_ref, piece_ref, *refs):
    mine_ref, theirs_ref, total_ref = refs[-3:]
    rows, width = own_ref.shape
    nz = len(offsets)
    nx = piece_ref.shape[0] // 2
    z, core = place_ref[0], place_ref[1]
    columns = []
    for chip in range(nx):
        for at, offset in enumerate(offsets):
            slot = lax.rem(z + (offset + nz), nz)
            start = pl.multiple_of(chip * (nz * share) + slot * share, share)
            columns.append((chip, at, pl.ds(start, share)))

    layers = ((own_ref, core), (other_ref, 1 - core))
    factors = []
    for index, (hidden_ref, layer) in enumerate(layers):
        partial = jnp.zeros((rows, share), F32)
        for chip, at, place in columns:
            slope = gain_ref[layer, :, place] * piece_ref[layer * nx + chip, at].astype(F32)
            partial += hidden_ref[:, place].astype(F32) * slope
        inv = inv_ref[index, :, :1]
        inner = jnp.sum(partial, axis=1, keepdims=True) * (1.0 / width)
        factors.append((inv, inv * inv * inner))
    for chip, at, place in columns:
        terms = []
        for (hidden_ref, layer), (inv, factor) in zip(layers, factors):
            slope = gain_ref[layer, :, place] * piece_ref[layer * nx + chip, at].astype(F32)
            terms.append((inv * (slope - hidden_ref[:, place].astype(F32) * factor)).astype(BF16))
        total = (terms[0].astype(F32) + terms[1].astype(F32)).astype(BF16)
        total_ref[:, place] = total
        mine_ref[:, place] = jnp.where(core > 0, terms[0], total)
        theirs_ref[:, place] = jnp.where(core > 0, total, terms[1])


def norm_backward(place, hidden, other, inv_pair, gain_pair, piece, offsets, after, share):
    half, width = other.shape[0] // 2, other.shape[1]
    rows = 32
    steps = half // rows
    half_block = pl.BlockSpec((rows, width), lambda i, at: (at[1] * steps + i, 0))
    row_block = pl.BlockSpec((rows, width), lambda i, at: (i, 0))

    def by_rows(array):
        return pl.BlockSpec((array.shape[0], rows, array.shape[2]), lambda i, at: (0, i, 0))

    return pl.pallas_call(
        functools.partial(term_kernel, share, offsets),
        grid_spec=pltpu.PrefetchScalarGridSpec(
            num_scalar_prefetch=1,
            grid=(steps,),
            in_specs=[half_block, half_block, by_rows(inv_pair), whole(*gain_pair.shape)]
            + [pl.BlockSpec(piece.shape[:2] + (rows, share), lambda i, at: (0, 0, i, 0))]
            + [ANY] * len(after),
            out_specs=(row_block,) * 3,
        ),
        out_shape=(pltpu.HBM((half, width), BF16),) * 3,
        compiler_params=params(16),
        cost_estimate=cost(20 * hidden.size, 4 * hidden.size),
        name="norm_backward",
    )(place, hidden, other, inv_pair, gain_pair, piece, *after)


def stream_kernel(core_ref, above_ref, sum_ref, *refs):
    refs[-1][...] = (above_ref[...].astype(F32) + sum_ref[...].astype(F32)).astype(BF16)


def stream_rows_kernel(core_ref, above_ref, sum_ref, whole_ref, out_ref):
    rows = out_ref.shape[0]
    span = pl.ds(pl.multiple_of(pl.program_id(0) * rows, rows), rows)
    out_ref[...] = (above_ref[span].astype(F32) + sum_ref[span].astype(F32)).astype(BF16)


def stream_half(core, above, within, into=None):
    half, width = above.shape
    rows = 16
    steps = half // rows
    own = into is None
    sources = [pl.BlockSpec((rows, width), lambda i, at: (i, 0)) if own else pl.BlockSpec(memory_space=pltpu.VMEM)] * 2
    return pl.pallas_call(
        stream_kernel if own else stream_rows_kernel,
        grid_spec=pltpu.PrefetchScalarGridSpec(
            num_scalar_prefetch=1,
            grid=(steps,),
            in_specs=sources + ([] if own else [HBM]),
            out_specs=pl.BlockSpec(
                (rows, width), lambda i, at: ((at[0] if own else 1 - at[0]) * steps + i, 0)
            ),
        ),
        out_shape=pltpu.HBM((2 * half, width), BF16),
        input_output_aliases={} if own else {3: 0},
        compiler_params=params(),
        cost_estimate=cost(above.size, 3 * above.size),
        name="stream_half",
    )(core, above, within, *([] if own else [into]))


def above_kernel(slices_ref, *refs):
    above_ref = refs[-1]
    chips = slices_ref.shape[0]
    running = jnp.zeros(slices_ref.shape[1:], F32)
    for chip in reversed(range(chips)):
        above_ref[chip] = running.astype(BF16)
        if chip:
            running += slices_ref[chip].astype(F32)


def sums_above(slices, after):
    chips, rows, width = slices.shape
    spec = pl.BlockSpec((chips, rows, width // 2), lambda i: (0, 0, i))
    return pl.pallas_call(
        above_kernel,
        grid=(2,),
        out_shape=pltpu.HBM(slices.shape, BF16),
        in_specs=[spec] + [ANY] * len(after),
        out_specs=spec,
        compiler_params=params(),
        cost_estimate=cost(slices.size, 2 * slices.size),
        name="sums_above",
    )(slices, *after)


def normalise_kernel(share, hidden_ref, gain_ref, out_ref):
    tokens, width = hidden_ref.shape
    squares = jnp.zeros((tokens, share), F32)
    for at in range(0, width, share):
        hidden = hidden_ref[:, at : at + share].astype(F32)
        squares += hidden * hidden
    inv = lax.rsqrt(jnp.sum(squares, axis=1, keepdims=True) * (1.0 / width) + EPS)
    for at in range(0, width, share):
        cols = slice(at, at + share)
        chip, place = divmod(at, out_ref.shape[2])
        normed = hidden_ref[:, cols].astype(F32) * inv * gain_ref[:, cols]
        out_ref[chip, :, place : place + share] = normed.astype(BF16)


def normalise(hidden, gain, share, nx):
    tokens, width = hidden.shape
    rows = 64
    return pl.pallas_call(
        functools.partial(normalise_kernel, share),
        grid=(tokens // rows,),
        out_shape=pltpu.HBM((nx, tokens, width // nx), BF16),
        in_specs=[pl.BlockSpec((rows, width), lambda i: (i, 0)), whole(*gain.shape)],
        out_specs=pl.BlockSpec((nx, rows, width // nx), lambda i: (0, i, 0)),
        compiler_params=params(),
        cost_estimate=cost(6 * hidden.size, 2 * hidden.size),
        name="normalise",
    )(hidden, gain)


def partials_kernel(share, offsets, nz, scale_factor, z_ref, masked_ref, normed_ref, b_ref, *refs):
    part_ref, projected_ref = refs[-2:]
    nx, tokens, key_width = masked_ref.shape
    lowrank = contract(masked_ref[...].reshape(nx * tokens, key_width), b_ref[...], (1, 1)).astype(BF16)
    for at in range(nz):
        normed = normed_ref[:, :, at * share : (at + 1) * share].reshape(nx * tokens, share)
        part_ref[at] = (scale_factor * contract(lowrank, normed, (0, 0))).astype(BF16)
    total = jnp.zeros(projected_ref.shape, F32)
    for ref, ref_offsets in zip(refs, offsets):
        for at, offset in enumerate(ref_offsets):
            slot = lax.rem(z_ref[0] + (offset + nz), nz)
            place = pl.ds(pl.multiple_of(slot * share, share), share)
            packed = ref[at]
            groups = packed.shape[1] // share
            a_cols = jnp.concatenate([packed[:, g * share : (g + 1) * share] for g in range(groups)], axis=0)
            total += contract(a_cols, normed_ref[:, :, place].reshape(nx * tokens, share), (1, 1))
    projected_ref[...] = total.astype(BF16)


def partials(z, masked_x, normed_x, b_mat, a_rows, offsets, after, share, nz, scale_factor):
    nx, tokens, _ = masked_x.shape
    rank = b_mat.shape[0]
    operands = (masked_x, normed_x, b_mat, *a_rows)
    shapes = ((nz, rank, share), (rank, nx * tokens))
    return pl.pallas_call(
        functools.partial(partials_kernel, share, offsets, nz, scale_factor),
        grid=(1,),
        out_shape=tuple(jax.ShapeDtypeStruct(shape, BF16) for shape in shapes),
        in_specs=[SMEM] + [whole(*operand.shape) for operand in operands] + [HBM] * len(after),
        out_specs=tuple(whole(*shape) for shape in shapes),
        compiler_params=params(16),
        cost_estimate=cost(4 * normed_x.size * rank, 2 * normed_x.size),
        name="partials",
    )(z, *operands, *after)


def partial_b_kernel(scale_factor, x_ref, masked_ref, *refs):
    parts, out_ref = refs[:-1], refs[-1]
    nx, tokens, _ = masked_ref.shape
    share = out_ref.shape[1]
    projected = parts[0][...].astype(F32)
    for part in parts[1:]:
        projected += part[...].astype(F32)
    place = pl.ds(pl.multiple_of(x_ref[0] * share, share), share)
    rows = masked_ref[:, :, place].reshape(nx * tokens, share)
    out_ref[...] = (scale_factor * contract(projected.astype(BF16), rows, (1, 0))).astype(BF16)


def partial_b(x, masked_x, parts, scale_factor):
    nx, _, key_width = masked_x.shape
    shape = (parts[0].shape[0], key_width // nx)
    return pl.pallas_call(
        functools.partial(partial_b_kernel, scale_factor),
        grid=(1,),
        out_shape=jax.ShapeDtypeStruct(shape, BF16),
        in_specs=[SMEM, whole(*masked_x.shape)] + [whole(*part.shape) for part in parts],
        out_specs=whole(*shape),
        compiler_params=params(),
        cost_estimate=cost(2 * masked_x.size * shape[0] // nx, masked_x.size),
        name="partial_b",
    )(x, masked_x, *parts)


def halves_kernel(side_ref, a_ref, b_ref, *refs):
    kept_ref, sent_ref = refs[-2:]
    half = kept_ref.shape[0]
    rank = a_ref.shape[1]
    for at in range(half):
        for out, begin in ((kept_ref, side_ref[0] * half), (sent_ref, (1 - side_ref[0]) * half)):
            out[at, :rank] = a_ref[begin + at]
            out[at, rank:] = b_ref[begin + at]


def halves(part_a, part_b, side, after):
    nz, rank, share = part_a.shape
    shape = (nz // 2, rank + part_b.shape[1], share)
    return pl.pallas_call(
        halves_kernel,
        grid=(1,),
        out_shape=(jax.ShapeDtypeStruct(shape, BF16),) * 2,
        in_specs=[SMEM, whole(*part_a.shape), whole(*part_b.shape)] + [HBM] * len(after),
        out_specs=(whole(*shape),) * 2,
        compiler_params=params(),
        cost_estimate=cost(0, 2 * part_a.size),
        name="halves",
    )(side, part_a, part_b, *after)


def add_kernel(count, side_ref, *refs):
    outs = refs[-1:] if refs[0].shape[0] == 1 else refs[-2:]
    half = outs[0].shape[0]
    for at in range(half):
        for out, begin in zip(outs, (side_ref[0] * half, (1 - side_ref[0]) * half)):
            where = begin + at if len(outs) == 2 else at
            total = refs[0][where].astype(F32)
            for ref in refs[1:count]:
                total += ref[where].astype(F32)
            out[at] = total.astype(out.dtype)


def add(values, side):
    shape = values[0].shape
    single = shape[0] == 1
    half = shape if single else (shape[0] // 2,) + shape[1:]
    out = jax.ShapeDtypeStruct(half, F32 if single else BF16)
    return pl.pallas_call(
        functools.partial(add_kernel, len(values)),
        grid=(1,),
        out_shape=(out,) * (1 if single else 2),
        in_specs=[SMEM] + [whole(*shape)] * len(values),
        out_specs=(whole(*half),) * (1 if single else 2),
        compiler_params=params(),
        cost_estimate=cost(len(values) * values[0].size, 4 * values[0].size),
        name="add",
    )(side, *values)


def scatter_begin(part_a, part_b, axis):
    bit = lax.axis_size(axis) // 2
    index = lax.axis_index(axis)
    kept, sent = halves(part_a, part_b, ((index // bit) % 2)[None], [])
    return add([kept, swap(sent, axis, bit)], ((index // (bit // 2)) % 2)[None])


def scatter_end(kept, sent, axis):
    bit = lax.axis_size(axis) // 4
    index = lax.axis_index(axis)
    while bit > 1:
        received = swap(sent, axis, bit)
        bit //= 2
        kept, sent = add([kept, received], ((index // bit) % 2)[None])
    return add([kept, swap(sent, axis, bit)], index[None])[0][0]


def shards(hidden_in, key_grad, key_weight, adapter_a, adapter_b, norm_gain, keep_flags, valid_counts):
    tokens, width = hidden_in.shape[1:]
    key_width = key_grad.shape[2]
    rank = adapter_a.shape[1]
    chips_y, cores = lax.axis_size("y"), lax.axis_size("core")
    nx, nz = lax.axis_size("x"), lax.axis_size("z")
    replicas = nx * nz
    half = tokens // cores
    share = width // replicas
    scale_factor = ADAPTER_SCALING / math.sqrt(tokens * replicas)
    x_index, z_index, core = (lax.axis_index(axis) for axis in ("x", "z", "core"))

    b_mat = in_hbm(adapter_b[0])
    block, masked = prepare(
        keep_flags[None], valid_counts[None], in_hbm(key_weight[0]), in_hbm(adapter_a[0]), b_mat, in_hbm(key_grad[0]), nx
    )
    masked_x = exchange(masked, "x")
    up, down = [block], [block]
    for step in range(1, nz // 2):
        up.append(shift(up[-1], "z", 1))
        down.append(shift(down[-1], "z", -1))
    up.append(shift(up[-1], "z", 1))

    hidden = in_hbm(hidden_in[0])
    other = swap(hidden, "core", 1)
    gain_pair = lax.all_gather(norm_gain, "core", axis=0, tiled=True)[:, None, :]

    rounds = [
        ([block, up[1], down[1]], [0, -1, 1], 0),
        ([up[2], down[2]], [-2, 2], 4),
        ([up[3], down[3]], [-3, 3], 6),
        ([up[4]], [-4], 3),
    ]
    normed_x = exchange(normalise(hidden, norm_gain, share, nx), "x")
    dnorm, a_rows = None, []
    for blocks, _, slot in rounds:
        dnorm, rows = products(
            masked_x,
            blocks,
            share,
            cores,
            nz,
            slot,
            into=dnorm,
            after=[normed_x] if slot == 6 else [],
        )
        a_rows.append(rows)
    a_offsets = [round_offsets for _, round_offsets, _ in rounds]
    offsets = [0, -1, 1, -4, -2, 2, -3, 3]
    dnorm = in_hbm(dnorm)
    piece = exchange(dnorm, ("core", "x"))

    part_a, projected = partials(
        z_index[None], masked_x, normed_x, b_mat, a_rows, a_offsets, [dnorm], share, nz, scale_factor
    )
    projected = [projected] + [shift(projected, "x", by) for by in (-1, 1, 2)]
    part_b = partial_b(x_index[None], masked_x, projected, scale_factor)
    part_b = part_b.reshape(rank, nz, key_width // replicas).transpose(1, 0, 2).reshape(nz, -1, share)
    inv_pair = inverses(core[None], hidden, other, [dnorm], share)
    mine, theirs, total = norm_backward(
        jnp.stack([z_index, core]), hidden, other, inv_pair, gain_pair, piece, offsets, [part_a], share
    )

    slices = exchange(total.reshape(chips_y, half // chips_y, width), "y")
    kept, sent = scatter_begin(part_a, part_b, "z")
    above_slices = sums_above(slices, [kept])
    beyond = swap(theirs, "core", 1)
    above = exchange(above_slices, "y").reshape(half, width)
    summed = scatter_end(kept, sent, "z")
    above, summed = lax.optimization_barrier((above, summed))
    received = swap(above, "core", 1)
    stream = stream_half(core[None], received, beyond, stream_half(core[None], above, mine))
    grad_a = summed[:rank]
    grad_b = summed[rank:].reshape(rank, key_width // replicas)
    return stream[None], grad_a[None], grad_b[None]


def solution(mesh):
    sections, replicas = mesh.devices.shape
    split = Mesh(mesh.devices.reshape(sections // 2, 2, 4, replicas // 4), ("y", "core", "x", "z"))
    section, dp = ("y", "core"), ("x", "z")
    return jax.shard_map(
        shards,
        mesh=split,
        in_specs=(
            P(section, dp, None),
            P(section, dp, None),
            P(section, dp, None),
            P(section, None, dp),
            P(section, None, None),
            P(section, None),
            P(section),
            P(dp),
        ),
        out_specs=(P(section, dp, None), P(section, None, dp), P(section, None, dp)),
        check_vma=False,
    )
```
